32 devices in a mesh: member: 2 (over x), space: 16 (over z, y, core).
Axes of the slice: x: 2, y: 2, z: 4, core: 2. Of those that a mesh axis runs over, the one named last changes fastest.
Arguments:
- tangents: float32 [8, 4, 48, 64, 128], P('member', None, 'space'), parts along dimension 0, may hold values from -210 to 210
- background: float32 [6, 4, 48, 64, 128], P('member', None, 'space'), parts along dimension 0, may hold values from -3 to 3
- diffusivity: float32 [4], P('member'), parts along dimension 0, may hold values from 0.03 to 0.12
Outputs:
- basis: float32 [8, 4, 48, 64, 128], P('member', None, 'space'), parts along dimension 0
- growth: float32 [8, 4], P('member'), parts along dimension 0
The draws below stay inside these ranges and needn't reach their ends.
There are 2 independent parts, one for each index of `member`. The reference program is written for one: setup_inputs(seed, part) draws one part's arguments, and reference() takes and returns one part's arrays. A program takes and returns all parts, laid end to end along the dimension named above; each array names one. Nothing has to cross between parts.
All inputs are finite; a program needn't handle non-finite values.
Results may differ from the reference program's by a relative error of at most 0.0003.
Values sent between devices are 32-bit elements; how exact they have to be, the bound alone decides.
A program may use at most 128 MiB of HBM per device.

```python
import math
import jax
import jax.numpy as jnp

VECTORS = 4
NX = 128
NY = 64
NZ = 48


def draw_tangents(key, part):
    key_noise = jax.random.fold_in(key, 11)
    key_scale = jax.random.fold_in(key, 12)
    shape = (VECTORS, 4, NZ, NY, NX)
    scales = jnp.exp(jax.random.uniform(key_scale, (VECTORS, 4, 1, 1, 1), jnp.float32, 0.0, math.log(10.0)))
    ramp = 1.0 + 2.0 * jnp.arange(NZ, dtype=jnp.float32) / max(NZ - 1, 1)
    ramp = ramp.reshape(1, 1, NZ, 1, 1)
    noise = jnp.clip(jax.random.normal(key_noise, shape, jnp.float32), -4.0, 4.0)
    return (noise * scales * ramp).astype(jnp.float32)


def levels(rng, dims, pieces, smallest, largest):
    def one(dim, shards_of):
        heights = jax.random.uniform(jax.random.fold_in(jax.random.fold_in(rng, 6), dim), (shards_of,), jnp.float32, smallest / len(pieces), largest / len(pieces))
        return jnp.repeat(jnp.exp(heights), dims[dim] // shards_of).reshape((-1,) + (1,) * (len(dims) - dim - 1))

    factor_of = one(*pieces[0])
    for cut in pieces[1:]:
        factor_of = factor_of * one(*cut)
    return factor_of


def bell_draw(own_key, dims, width, bound, cuts=(), kind=jnp.bfloat16):
    loudness = levels(own_key, dims, cuts, -0.22, 0.18) if cuts else 1.0
    values = jax.random.normal(own_key, dims, jnp.float32) * width * loudness
    return jnp.minimum(jnp.maximum(values, -bound), bound).astype(kind)


def setup_inputs(seed: int = 0, part: int = 0) -> dict:
    keys = jax.random.split(jax.random.key(seed), 4)
    part_splits = jax.random.split(jax.random.fold_in(keys[3], part), 4)
    return {
        "tangents": draw_tangents(jax.random.fold_in(jax.random.fold_in(keys[3], part), 71), part),
        "background": bell_draw(part_splits[1], (3, 4, NZ, NY, NX), 0.5, 3.0, ((2, 16),), jnp.float32),
        "diffusivity": jnp.clip(jnp.exp(jax.random.uniform(part_splits[2], (2,), jnp.float32, math.log(0.03), math.log(0.12))), 0.03, 0.12),
    }


STEP_DT = 0.25
BUOYANCY = 1.0

def inner(field):
    return field[..., 1:-1, :, :]

def slopes(field):
    slope_x = inner(jnp.roll(field, -1, axis=-1) - jnp.roll(field, 1, axis=-1)) * 0.5
    slope_y = inner(jnp.roll(field, -1, axis=-2) - jnp.roll(field, 1, axis=-2)) * 0.5
    slope_z = (field[..., 2:, :, :] - field[..., :-2, :, :]) * 0.5
    return (slope_x, slope_y, slope_z)

def laplace(field):
    sides = jnp.roll(field, -1, axis=-1) + jnp.roll(field, 1, axis=-1)
    sides = sides + jnp.roll(field, -1, axis=-2) + jnp.roll(field, 1, axis=-2)
    return inner(sides) + field[..., 2:, :, :] + field[..., :-2, :, :] - 6.0 * inner(field)

def tendency(tangent, ground, viscous, conduct):
    base_x, base_y, base_z = slopes(ground)
    flow = inner(ground)
    own_x, own_y, own_z = slopes(tangent)
    advect = flow[0] * own_x + flow[1] * own_y + flow[2] * own_z
    moving = inner(tangent)
    shear = moving[:, 0:1] * base_x[None] + moving[:, 1:2] * base_y[None] + moving[:, 2:3] * base_z[None]
    coeffs = jnp.stack([viscous, viscous, viscous, conduct]).reshape(4, 1, 1, 1)
    zeros = jnp.zeros_like(moving[:, 0:2])
    forcing = jnp.concatenate([zeros, BUOYANCY * moving[:, 3:4], moving[:, 2:3]], axis=1)
    return -advect - shear + coeffs * laplace(tangent) + forcing

def padded(field):
    widths = [(0, 0)] * (field.ndim - 3) + [(1, 1), (0, 0), (0, 0)]
    return jnp.pad(field, widths)

def reference(tangents, background, diffusivity):
    viscous = diffusivity[0]
    conduct = diffusivity[1]
    rate_one = tendency(padded(tangents), padded(background[0]), viscous, conduct)
    first = tangents + STEP_DT * 0.5 * rate_one
    rate_two = tendency(padded(first), padded(background[1]), viscous, conduct)
    second = tangents + STEP_DT * 0.5 * rate_two
    rate_three = tendency(padded(second), padded(background[1]), viscous, conduct)
    third = tangents + STEP_DT * rate_three
    rate_four = tendency(padded(third), padded(background[2]), viscous, conduct)
    stepped = tangents + STEP_DT / 6.0 * (rate_one + 2.0 * rate_two + 2.0 * rate_three + rate_four)
    count = stepped.shape[0]
    matrix = stepped.reshape(count, -1).T
    ortho, factor = jnp.linalg.qr(matrix)
    signs = jnp.sign(jnp.diagonal(factor))
    ortho = ortho * signs[None, :]
    factor = factor * signs[:, None]
    scale = jnp.sqrt(jnp.float32(matrix.shape[0]))
    basis = (ortho.T * scale).reshape(stepped.shape)
    return (basis, factor / scale)
```

```python
import functools
import jax
import jax.numpy as jnp
from jax import lax
from jax.experimental import pallas as pl
from jax.experimental.pallas import tpu as pltpu
from jax.sharding import PartitionSpec as P

STEP_DT = 0.25
BUOYANCY = 1.0
MESH = pl.DeviceIdType.MESH
PAD = 8
ROWS = 16
PAIRS = [(i, j) for j in range(4) for i in range(j + 1)]


def step_kernel(
    space,
    t_hbm,
    b_hbm,
    diff,
    stepped,
    coef_out,
    y0,
    y1,
    y2,
    y3,
    base,
    base_lo,
    base_hi,
    lo,
    hi,
    coef,
    grams,
    local_sem,
    send_sem,
    recv_sem,
    base_send,
    base_recv,
    gram_send,
    gram_recv,
):
    vectors, comps, depth, ny, nx = t_hbm.shape
    states = b_hbm.shape[0]
    last = depth - 1
    me = lax.axis_index("space")
    upper = lax.rem(me + 1, space)
    lower = lax.rem(me + space - 1, space)
    has_lower = me > 0
    has_upper = me < space - 1
    ys = [y0, y1, y2, y3]
    nu, kappa = diff[0], diff[1]

    def local_copies():
        out = []
        for k, (src, dst) in enumerate(((b_hbm, base), (t_hbm, y0))):
            for m, (a, b, rows) in enumerate(
                ((0, PAD, ny), (ny - PAD, 0, PAD), (0, PAD + ny, PAD))
            ):
                out.append(
                    pltpu.make_async_copy(
                        src.at[:, :, :, pl.ds(a, rows), :],
                        dst.at[:, :, :, pl.ds(b, rows), :],
                        local_sem.at[k, m],
                    )
                )
        return out

    def base_up(b):
        return pltpu.make_async_remote_copy(
            b_hbm.at[b, :, last], base_lo.at[b], base_send.at[0, b], base_recv.at[0, b],
            device_id={"space": upper}, device_id_type=MESH,
        )

    def base_down(b):
        return pltpu.make_async_remote_copy(
            b_hbm.at[b, :, 0], base_hi.at[b], base_send.at[1, b], base_recv.at[1, b],
            device_id={"space": lower}, device_id_type=MESH,
        )

    def state_plane(s, j, p):
        if s == 0:
            return t_hbm.at[j, :, p]
        return ys[s].at[j, :, p, pl.ds(PAD, ny), :]

    def send_up(s, j):
        return pltpu.make_async_remote_copy(
            state_plane(s, j, last), lo.at[s, j], send_sem.at[0, s, j], recv_sem.at[0, s, j],
            device_id={"space": upper}, device_id_type=MESH,
        )

    def send_down(s, j):
        return pltpu.make_async_remote_copy(
            state_plane(s, j, 0), hi.at[s, j], send_sem.at[1, s, j], recv_sem.at[1, s, j],
            device_id={"space": lower}, device_id_type=MESH,
        )

    def both(up, down, *key, op):
        @pl.when(has_upper)
        def _():
            getattr(up(*key), op)()

        @pl.when(has_lower)
        def _():
            getattr(down(*key), op)()

    def receive(up, down, *key):
        @pl.when(has_lower)
        def _():
            up(*key).wait_recv()

        @pl.when(has_upper)
        def _():
            down(*key).wait_recv()

    copies = local_copies()
    for c in copies:
        c.start()

    barrier = pltpu.get_barrier_semaphore()

    @pl.loop(1, space)
    def _(d):
        pl.semaphore_signal(
            barrier, inc=1, device_id={"space": lax.rem(me + d, space)}, device_id_type=MESH
        )

    pl.semaphore_wait(barrier, space - 1)

    both(base_up, base_down, 0, op="start")

    @pl.loop(0, vectors)
    def _(j):
        both(send_up, send_down, 0, j, op="start")

    both(base_up, base_down, 1, op="start")

    @pl.when(jnp.logical_not(has_lower))
    def _():
        base_lo[...] = jnp.zeros_like(base_lo)

        @pl.loop(0, vectors)
        def _(j):
            for s in range(4):
                lo[s, j] = jnp.zeros(lo.shape[2:], jnp.float32)

    @pl.when(jnp.logical_not(has_upper))
    def _():
        base_hi[...] = jnp.zeros_like(base_hi)

        @pl.loop(0, vectors)
        def _(j):
            for s in range(4):
                hi[s, j] = jnp.zeros(hi.shape[2:], jnp.float32)

    for c in copies:
        c.wait()

    def x_sides(q):
        return pltpu.roll(q, nx - 1, 1), pltpu.roll(q, 1, 1)

    def base_coeffs(b, p):
        @pl.loop(0, ny, step=ROWS)
        def _(r):
            r = pl.multiple_of(r, ROWS)
            here = pl.ds(r, ROWS)
            for c in range(comps):
                q = base[b, c, p, pl.ds(PAD + r, ROWS), :]
                right, left = x_sides(q)
                front = base[b, c, p, pl.ds(PAD + 1 + r, ROWS), :]
                back = base[b, c, p, pl.ds(PAD - 1 + r, ROWS), :]
                if p == 0:
                    below = base_lo[b, c, here, :]
                else:
                    below = base[b, c, p - 1, pl.ds(PAD + r, ROWS), :]
                if p == last:
                    above = base_hi[b, c, here, :]
                else:
                    above = base[b, c, p + 1, pl.ds(PAD + r, ROWS), :]
                if c < 3:
                    coef[b, p, c, here, :] = -0.5 * q
                coef[b, p, 3 + 3 * c, here, :] = 0.5 * (left - right)
                coef[b, p, 4 + 3 * c, here, :] = 0.5 * (back - front)
                coef[b, p, 5 + 3 * c, here, :] = 0.5 * (below - above)

    def advance(s, b, j, p):
        y = ys[s]

        @pl.loop(0, ny, step=ROWS)
        def _(r):
            r = pl.multiple_of(r, ROWS)
            here = pl.ds(r, ROWS)
            mid = pl.ds(PAD + r, ROWS)
            qs = [y[j, c, p, mid, :] for c in range(comps)]
            flow = [coef[b, p, d, here, :] for d in range(3)]
            for c in range(comps):
                q = qs[c]
                right, left = x_sides(q)
                front = y[j, c, p, pl.ds(PAD + 1 + r, ROWS), :]
                back = y[j, c, p, pl.ds(PAD - 1 + r, ROWS), :]
                below = lo[s, j, c, here, :] if p == 0 else y[j, c, p - 1, mid, :]
                above = hi[s, j, c, here, :] if p == last else y[j, c, p + 1, mid, :]
                rate = (
                    flow[0] * (right - left) + flow[1] * (front - back) + flow[2] * (above - below)
                )
                for d in range(3):
                    rate = rate + qs[d] * coef[b, p, 3 + 3 * c + d, here, :]
                around = (right + left) + (front + back) + (above + below)
                rate = rate + (kappa if c == 3 else nu) * (around - 6.0 * q)
                if c == 2:
                    rate = rate + BUOYANCY * qs[3]
                if c == 3:
                    rate = rate + qs[2]
                if s < 3:
                    start = q if s == 0 else y0[j, c, p, mid, :]
                    step = STEP_DT if s == 2 else STEP_DT * 0.5
                    ys[s + 1][j, c, p, mid, :] = start + step * rate
                else:
                    sums = (
                        y1[j, c, p, mid, :] + 2.0 * y2[j, c, p, mid, :] + (q - y0[j, c, p, mid, :])
                    )
                    stepped[j, c, p, here, :] = (1.0 / 3.0) * sums + (STEP_DT / 6.0) * rate

        if s < 3:
            nxt = ys[s + 1]
            for c in range(comps):
                nxt[j, c, p, pl.ds(0, PAD), :] = nxt[j, c, p, pl.ds(ny, PAD), :]
                nxt[j, c, p, pl.ds(PAD + ny, PAD), :] = nxt[j, c, p, pl.ds(PAD, PAD), :]

    inside = range(1, last)
    outside = [0, last] if last > 0 else [0]

    for p in inside:
        base_coeffs(0, p)
    receive(base_up, base_down, 0)
    for p in outside:
        base_coeffs(0, p)

    which = [0, 1, 1, 2]
    for s in range(4):
        if s == 1:
            receive(base_up, base_down, 1)
            for p in range(depth):
                base_coeffs(1, p)
        if s == 3:
            receive(base_up, base_down, 2)
            for p in range(depth):
                base_coeffs(2, p)

        @pl.loop(0, vectors)
        def _(j):
            receive(send_up, send_down, s, j)
            for p in outside:
                advance(s, which[s], j, p)
            if s < 3:
                both(send_up, send_down, s + 1, j, op="start")
            for p in inside:
                advance(s, which[s], j, p)

        if s == 1:
            both(base_up, base_down, 2, op="start")

    zero = jnp.zeros((ROWS, nx), jnp.float32)
    sums = (zero,) * len(PAIRS)
    for p in range(depth):
        def body(k, sums, p=p):
            r = pl.multiple_of(k * ROWS, ROWS)
            for c in range(comps):
                q = [stepped[j, c, p, pl.ds(r, ROWS), :] for j in range(vectors)]
                sums = tuple(a + q[i] * q[j] for a, (i, j) in zip(sums, PAIRS))
            return sums

        sums = lax.fori_loop(0, ny // ROWS, body, sums)
    rows = [jnp.sum(a, axis=0, keepdims=True) for a in sums]
    rows += [jnp.zeros((1, nx), jnp.float32)] * (16 - len(rows))
    grams[me] = jnp.concatenate(rows, axis=0)

    def gram_copy(d):
        return pltpu.make_async_remote_copy(
            grams.at[me], grams.at[me], gram_send.at[d], gram_recv.at[d],
            device_id={"space": lax.rem(me + d, space)}, device_id_type=MESH,
        )

    def gram_arrival(d):
        source = lax.rem(me + space - d, space)
        return pltpu.make_async_remote_copy(
            grams.at[source], grams.at[source], gram_send.at[d], gram_recv.at[d],
            device_id={"space": lax.rem(me + d, space)}, device_id_type=MESH,
        )

    @pl.loop(1, space)
    def _(d):
        gram_copy(d).start()

    @pl.loop(1, space)
    def _(d):
        gram_arrival(d).wait_recv()

    total = lax.fori_loop(0, space, lambda d, a: a + grams[d], jnp.zeros((16, nx), jnp.float32))
    total = jnp.broadcast_to(jnp.sum(total, axis=1, keepdims=True), (16, nx))
    gram = {pair: total[k : k + 1, :] for k, pair in enumerate(PAIRS)}

    low, inv = {}, {}
    recip = {}
    for k in range(vectors):
        rest = gram[k, k]
        for m in range(k):
            rest = rest - low[k, m] * low[k, m]
        low[k, k] = jnp.sqrt(rest)
        recip[k] = 1.0 / low[k, k]
        for i in range(k + 1, vectors):
            rest = gram[k, i]
            for m in range(k):
                rest = rest - low[i, m] * low[k, m]
            low[i, k] = rest * recip[k]
    for k in range(vectors):
        inv[k, k] = recip[k]
        for i in range(k + 1, vectors):
            rest = low[i, k] * inv[k, k]
            for m in range(k + 1, i):
                rest = rest + low[i, m] * inv[m, k]
            inv[i, k] = -rest * recip[i]
    blank = jnp.zeros((1, nx), jnp.float32)
    rows = [inv.get((i, k), blank) for i in range(vectors) for k in range(vectors)]
    rows += [low.get((k, i), blank) for i in range(vectors) for k in range(vectors)]
    coef_out[...] = jnp.concatenate(rows, axis=0)

    for b in range(states):
        both(base_up, base_down, b, op="wait_send")
    for s in range(4):
        @pl.loop(0, vectors)
        def _(j):
            both(send_up, send_down, s, j, op="wait_send")

    @pl.loop(1, space)
    def _(d):
        gram_copy(d).wait_send()


def basis_kernel(count, stepped, coef, basis, growth):
    vectors, _, depth, ny, nx = stepped.shape
    scale = jnp.sqrt(jnp.float32(count))
    comp = pl.program_id(0)

    def row(k):
        return jnp.broadcast_to(coef[k : k + 1, :], (8, nx))

    mix = {(i, k): scale * row(i * vectors + k) for i in range(vectors) for k in range(i + 1)}
    for p in range(depth):
        for r in range(0, ny, 8):
            q = [stepped[k, comp, p, r : r + 8, :] for k in range(vectors)]
            for i in range(vectors):
                total = mix[i, 0] * q[0]
                for k in range(1, i + 1):
                    total = total + mix[i, k] * q[k]
                basis[i, 0, p, r : r + 8, :] = total

    @pl.when(comp == 0)
    def _():
        lane = lax.broadcasted_iota(jnp.int32, (1, nx), 1)
        rows = []
        for i in range(vectors):
            out = jnp.zeros((1, nx), jnp.float32)
            for k in range(vectors):
                at = vectors * vectors + i * vectors + k
                out = jnp.where(lane == k, coef[at : at + 1, :], out)
            rows.append(out)
        growth[...] = (jnp.concatenate(rows, axis=0) / scale)[:, :vectors]


def on_device(tangents, background, diffusivity):
    space = lax.axis_size("space")
    vectors, comps, depth, ny, nx = tangents.shape
    states = background.shape[0]
    f32 = jnp.float32
    padded = ny + 2 * PAD
    vmem = pl.BlockSpec(memory_space=pltpu.VMEM)
    hbm = pl.BlockSpec(memory_space=pl.ANY)
    stepped, coef = pl.pallas_call(
        functools.partial(step_kernel, space),
        out_shape=(
            jax.ShapeDtypeStruct(tangents.shape, f32),
            jax.ShapeDtypeStruct((2 * vectors * vectors, nx), f32),
        ),
        in_specs=[hbm, hbm, pl.BlockSpec(memory_space=pltpu.SMEM)],
        out_specs=(vmem, vmem),
        scratch_shapes=[pltpu.VMEM((vectors, comps, depth, padded, nx), f32)] * 4
        + [
            pltpu.VMEM((states, comps, depth, padded, nx), f32),
            pltpu.VMEM((states, comps, ny, nx), f32),
            pltpu.VMEM((states, comps, ny, nx), f32),
            pltpu.VMEM((4, vectors, comps, ny, nx), f32),
            pltpu.VMEM((4, vectors, comps, ny, nx), f32),
            pltpu.VMEM((states, depth, 15, ny, nx), f32),
            pltpu.VMEM((space, 16, nx), f32),
            pltpu.SemaphoreType.DMA((2, 3)),
            pltpu.SemaphoreType.DMA((2, 4, vectors)),
            pltpu.SemaphoreType.DMA((2, 4, vectors)),
            pltpu.SemaphoreType.DMA((2, states)),
            pltpu.SemaphoreType.DMA((2, states)),
            pltpu.SemaphoreType.DMA((space,)),
            pltpu.SemaphoreType.DMA((space,)),
        ],
        compiler_params=pltpu.CompilerParams(
            collective_id=0, has_side_effects=True, vmem_limit_bytes=48 * 1024 * 1024
        ),
        name="tangent_step",
    )(tangents, background, diffusivity)
    block = (vectors, 1, depth, ny, nx)
    return pl.pallas_call(
        functools.partial(basis_kernel, tangents[0].size * space),
        grid=(comps,),
        out_shape=(
            jax.ShapeDtypeStruct(tangents.shape, f32),
            jax.ShapeDtypeStruct((vectors, vectors), f32),
        ),
        in_specs=[vmem, vmem],
        out_specs=(pl.BlockSpec(block, lambda c: (0, c, 0, 0, 0)), vmem),
        compiler_params=pltpu.CompilerParams(vmem_limit_bytes=16 * 1024 * 1024),
        name="basis",
    )(stepped, coef)


def solution(mesh):
    in_specs = (
        P("member", None, "space", None, None),
        P("member", None, "space", None, None),
        P("member"),
    )
    out_specs = (P("member", None, "space", None, None), P("member", None))
    return jax.shard_map(
        on_device, mesh=mesh, in_specs=in_specs, out_specs=out_specs, check_vma=False
    )
```

```python
import functools
import jax
import jax.numpy as jnp
from jax import lax
from jax.experimental import pallas as pl
from jax.experimental.pallas import tpu as pltpu
from jax.sharding import PartitionSpec as P

STEP_DT = 0.25
BUOYANCY = 1.0
MESH = pl.DeviceIdType.MESH
PAD = 8
ROWS = 32
GRAM_ROWS = 16
PAIRS = [(i, j) for j in range(4) for i in range(j + 1)]


def step_kernel(
    space,
    t_hbm,
    b_hbm,
    diff_hbm,
    stepped,
    coef_out,
    y0,
    y1,
    y2,
    y3,
    base,
    base_lo,
    base_hi,
    lo,
    hi,
    coef,
    grams,
    diff,
    local_sem,
    send_sem,
    recv_sem,
    base_send,
    base_recv,
    gram_send,
    gram_recv,
):
    vectors, comps, depth, ny, nx = t_hbm.shape
    states = b_hbm.shape[0]
    last = depth - 1
    me = lax.axis_index("space")
    upper = lax.rem(me + 1, space)
    lower = lax.rem(me + space - 1, space)
    has_lower = me > 0
    has_upper = me < space - 1
    ys = [y0, y1, y2, y3]

    def local_copies():
        out = []
        for k, (src, dst) in enumerate(((b_hbm, base), (t_hbm, y0))):
            for m, (a, b, rows) in enumerate(
                ((0, PAD, ny), (ny - PAD, 0, PAD), (0, PAD + ny, PAD))
            ):
                out.append(
                    pltpu.make_async_copy(
                        src.at[:, :, :, pl.ds(a, rows), :],
                        dst.at[:, :, :, pl.ds(b, rows), :],
                        local_sem.at[k, m],
                    )
                )
        return out

    def base_up(b):
        return pltpu.make_async_remote_copy(
            b_hbm.at[b, :, last], base_lo.at[b], base_send.at[0, b], base_recv.at[0, b],
            device_id={"space": upper}, device_id_type=MESH,
        )

    def base_down(b):
        return pltpu.make_async_remote_copy(
            b_hbm.at[b, :, 0], base_hi.at[b], base_send.at[1, b], base_recv.at[1, b],
            device_id={"space": lower}, device_id_type=MESH,
        )

    def state_plane(s, j, p):
        if s == 0:
            return t_hbm.at[j, :, p]
        return ys[s].at[j, :, p, pl.ds(PAD, ny), :]

    def send_up(s, j):
        return pltpu.make_async_remote_copy(
            state_plane(s, j, last), lo.at[s, j], send_sem.at[0, s, j], recv_sem.at[0, s, j],
            device_id={"space": upper}, device_id_type=MESH,
        )

    def send_down(s, j):
        return pltpu.make_async_remote_copy(
            state_plane(s, j, 0), hi.at[s, j], send_sem.at[1, s, j], recv_sem.at[1, s, j],
            device_id={"space": lower}, device_id_type=MESH,
        )

    def both(up, down, *key, op):
        @pl.when(has_upper)
        def _():
            getattr(up(*key), op)()

        @pl.when(has_lower)
        def _():
            getattr(down(*key), op)()

    def receive(up, down, *key):
        @pl.when(has_lower)
        def _():
            up(*key).wait_recv()

        @pl.when(has_upper)
        def _():
            down(*key).wait_recv()

    copies = local_copies() + [pltpu.make_async_copy(diff_hbm, diff, local_sem.at[2, 0])]
    for c in copies:
        c.start()

    barrier = pltpu.get_barrier_semaphore()

    @pl.loop(1, space)
    def _(d):
        pl.semaphore_signal(
            barrier, inc=1, device_id={"space": lax.rem(me + d, space)}, device_id_type=MESH
        )

    pl.semaphore_wait(barrier, space - 1)

    both(base_up, base_down, 0, op="start")

    @pl.loop(0, vectors)
    def _(j):
        both(send_up, send_down, 0, j, op="start")

    both(base_up, base_down, 1, op="start")

    @pl.when(jnp.logical_not(has_lower))
    def _():
        base_lo[...] = jnp.zeros_like(base_lo)

        @pl.loop(0, vectors)
        def _(j):
            for s in range(4):
                lo[s, j] = jnp.zeros(lo.shape[2:], jnp.float32)

    @pl.when(jnp.logical_not(has_upper))
    def _():
        base_hi[...] = jnp.zeros_like(base_hi)

        @pl.loop(0, vectors)
        def _(j):
            for s in range(4):
                hi[s, j] = jnp.zeros(hi.shape[2:], jnp.float32)

    for c in copies:
        c.wait()
    nu, kappa = diff[0], diff[1]

    def x_sides(q):
        return pltpu.roll(q, nx - 1, 1), pltpu.roll(q, 1, 1)

    def base_coeffs(b, p):
        @pl.loop(0, ny, step=ROWS)
        def _(r):
            r = pl.multiple_of(r, ROWS)
            here = pl.ds(r, ROWS)
            for c in range(comps):
                q = base[b, c, p, pl.ds(PAD + r, ROWS), :]
                right, left = x_sides(q)
                front = base[b, c, p, pl.ds(PAD + 1 + r, ROWS), :]
                back = base[b, c, p, pl.ds(PAD - 1 + r, ROWS), :]
                if p == 0:
                    below = base_lo[b, c, here, :]
                else:
                    below = base[b, c, p - 1, pl.ds(PAD + r, ROWS), :]
                if p == last:
                    above = base_hi[b, c, here, :]
                else:
                    above = base[b, c, p + 1, pl.ds(PAD + r, ROWS), :]
                if c < 3:
                    coef[b, p, c, here, :] = -0.5 * q
                coef[b, p, 3 + 3 * c, here, :] = 0.5 * (left - right)
                coef[b, p, 4 + 3 * c, here, :] = 0.5 * (back - front)
                coef[b, p, 5 + 3 * c, here, :] = 0.5 * (below - above)

    def advance(s, b, j, p):
        y = ys[s]

        @pl.loop(0, ny, step=ROWS)
        def _(r):
            r = pl.multiple_of(r, ROWS)
            here = pl.ds(r, ROWS)
            mid = pl.ds(PAD + r, ROWS)
            qs = [y[j, c, p, mid, :] for c in range(comps)]
            flow = [coef[b, p, d, here, :] for d in range(3)]
            for c in range(comps):
                q = qs[c]
                right, left = x_sides(q)
                front = y[j, c, p, pl.ds(PAD + 1 + r, ROWS), :]
                back = y[j, c, p, pl.ds(PAD - 1 + r, ROWS), :]
                below = lo[s, j, c, here, :] if p == 0 else y[j, c, p - 1, mid, :]
                above = hi[s, j, c, here, :] if p == last else y[j, c, p + 1, mid, :]
                rate = (
                    flow[0] * (right - left) + flow[1] * (front - back) + flow[2] * (above - below)
                )
                for d in range(3):
                    rate = rate + qs[d] * coef[b, p, 3 + 3 * c + d, here, :]
                around = (right + left) + (front + back) + (above + below)
                rate = rate + (kappa if c == 3 else nu) * (around - 6.0 * q)
                if c == 2:
                    rate = rate + BUOYANCY * qs[3]
                if c == 3:
                    rate = rate + qs[2]
                if s < 3:
                    start = q if s == 0 else y0[j, c, p, mid, :]
                    step = STEP_DT if s == 2 else STEP_DT * 0.5
                    ys[s + 1][j, c, p, mid, :] = start + step * rate
                else:
                    sums = (
                        y1[j, c, p, mid, :] + 2.0 * y2[j, c, p, mid, :] + (q - y0[j, c, p, mid, :])
                    )
                    stepped[j, c, p, here, :] = (1.0 / 3.0) * sums + (STEP_DT / 6.0) * rate

        if s < 3:
            nxt = ys[s + 1]
            for c in range(comps):
                nxt[j, c, p, pl.ds(0, PAD), :] = nxt[j, c, p, pl.ds(ny, PAD), :]
                nxt[j, c, p, pl.ds(PAD + ny, PAD), :] = nxt[j, c, p, pl.ds(PAD, PAD), :]

    inside = range(1, last)
    outside = [0, last] if last > 0 else [0]

    for p in inside:
        base_coeffs(0, p)

    which = [0, 1, 1, 2]
    for s in range(4):
        early = s in (0, 3)
        if early:

            @pl.loop(0, vectors)
            def _(j):
                for p in inside:
                    advance(s, which[s], j, p)

        if s == 0:
            for b in range(1, states):
                for p in inside:
                    base_coeffs(b, p)
        if s != 2:
            receive(base_up, base_down, which[s])
            for p in outside:
                base_coeffs(which[s], p)

        @pl.loop(0, vectors)
        def _(j):
            receive(send_up, send_down, s, j)
            for p in outside:
                advance(s, which[s], j, p)
            if s < 3:
                both(send_up, send_down, s + 1, j, op="start")
            if not early:
                for p in inside:
                    advance(s, which[s], j, p)

        if s == 1:
            both(base_up, base_down, 2, op="start")

    zero = jnp.zeros((GRAM_ROWS, nx), jnp.float32)
    sums = (zero,) * len(PAIRS)
    for p in range(depth):
        def body(k, sums, p=p):
            r = pl.multiple_of(k * GRAM_ROWS, GRAM_ROWS)
            for c in range(comps):
                q = [stepped[j, c, p, pl.ds(r, GRAM_ROWS), :] for j in range(vectors)]
                sums = tuple(a + q[i] * q[j] for a, (i, j) in zip(sums, PAIRS))
            return sums

        sums = lax.fori_loop(0, ny // GRAM_ROWS, body, sums)
    lane = lax.broadcasted_iota(jnp.int32, (1, nx), 1)
    packed = jnp.zeros((1, nx), jnp.float32)
    for k, a in enumerate(sums):
        whole = jnp.sum(jnp.sum(a, axis=0, keepdims=True), axis=1, keepdims=True)
        packed = jnp.where(lane == k, whole, packed)
    grams[me] = packed

    def gram_copy(d):
        return pltpu.make_async_remote_copy(
            grams.at[me], grams.at[me], gram_send.at[d], gram_recv.at[d],
            device_id={"space": lax.rem(me + d, space)}, device_id_type=MESH,
        )

    def gram_arrival(d):
        source = lax.rem(me + space - d, space)
        return pltpu.make_async_remote_copy(
            grams.at[source], grams.at[source], gram_send.at[d], gram_recv.at[d],
            device_id={"space": lax.rem(me + d, space)}, device_id_type=MESH,
        )

    @pl.loop(1, space)
    def _(d):
        gram_copy(d).start()

    @pl.loop(1, space)
    def _(d):
        gram_arrival(d).wait_recv()

    total = lax.fori_loop(0, space, lambda d, a: a + grams[d], jnp.zeros((1, nx), jnp.float32))
    gram = {
        pair: jnp.broadcast_to(
            jnp.sum(jnp.where(lane == k, total, 0.0), axis=1, keepdims=True), (1, nx)
        )
        for k, pair in enumerate(PAIRS)
    }

    low, inv = {}, {}
    recip = {}
    for k in range(vectors):
        rest = gram[k, k]
        for m in range(k):
            rest = rest - low[k, m] * low[k, m]
        low[k, k] = jnp.sqrt(rest)
        recip[k] = 1.0 / low[k, k]
        for i in range(k + 1, vectors):
            rest = gram[k, i]
            for m in range(k):
                rest = rest - low[i, m] * low[k, m]
            low[i, k] = rest * recip[k]
    for k in range(vectors):
        inv[k, k] = recip[k]
        for i in range(k + 1, vectors):
            rest = low[i, k] * inv[k, k]
            for m in range(k + 1, i):
                rest = rest + low[i, m] * inv[m, k]
            inv[i, k] = -rest * recip[i]
    blank = jnp.zeros((1, nx), jnp.float32)
    rows = [inv.get((i, k), blank) for i in range(vectors) for k in range(vectors)]
    rows += [low.get((k, i), blank) for i in range(vectors) for k in range(vectors)]
    coef_out[...] = jnp.concatenate(rows, axis=0)

    for b in range(states):
        both(base_up, base_down, b, op="wait_send")
    for s in range(4):
        @pl.loop(0, vectors)
        def _(j):
            both(send_up, send_down, s, j, op="wait_send")

    @pl.loop(1, space)
    def _(d):
        gram_copy(d).wait_send()


def basis_kernel(count, stepped, coef, basis, growth):
    vectors, _, depth, ny, nx = stepped.shape
    scale = jnp.sqrt(jnp.float32(count))
    comp = pl.program_id(0)

    def row(k):
        return jnp.broadcast_to(coef[k : k + 1, :], (8, nx))

    mix = {(i, k): scale * row(i * vectors + k) for i in range(vectors) for k in range(i + 1)}
    for p in range(depth):
        for r in range(0, ny, 8):
            q = [stepped[k, comp, p, r : r + 8, :] for k in range(vectors)]
            for i in range(vectors):
                total = mix[i, 0] * q[0]
                for k in range(1, i + 1):
                    total = total + mix[i, k] * q[k]
                basis[i, 0, p, r : r + 8, :] = total

    @pl.when(comp == 0)
    def _():
        lane = lax.broadcasted_iota(jnp.int32, (1, nx), 1)
        rows = []
        for i in range(vectors):
            out = jnp.zeros((1, nx), jnp.float32)
            for k in range(vectors):
                at = vectors * vectors + i * vectors + k
                out = jnp.where(lane == k, coef[at : at + 1, :], out)
            rows.append(out)
        growth[...] = (jnp.concatenate(rows, axis=0) / scale)[:, :vectors]


def on_device(tangents, background, diffusivity):
    space = lax.axis_size("space")
    vectors, comps, depth, ny, nx = tangents.shape
    states = background.shape[0]
    f32 = jnp.float32
    padded = ny + 2 * PAD
    vmem = pl.BlockSpec(memory_space=pltpu.VMEM)
    hbm = pl.BlockSpec(memory_space=pltpu.HBM)
    stepped, coef = pl.pallas_call(
        functools.partial(step_kernel, space),
        out_shape=(
            jax.ShapeDtypeStruct(tangents.shape, f32),
            jax.ShapeDtypeStruct((2 * vectors * vectors, nx), f32),
        ),
        in_specs=[hbm, hbm, hbm],
        out_specs=(vmem, vmem),
        scratch_shapes=[pltpu.VMEM((vectors, comps, depth, padded, nx), f32)] * 4
        + [
            pltpu.VMEM((states, comps, depth, padded, nx), f32),
            pltpu.VMEM((states, comps, ny, nx), f32),
            pltpu.VMEM((states, comps, ny, nx), f32),
            pltpu.VMEM((4, vectors, comps, ny, nx), f32),
            pltpu.VMEM((4, vectors, comps, ny, nx), f32),
            pltpu.VMEM((states, depth, 15, ny, nx), f32),
            pltpu.VMEM((space, 1, nx), f32),
            pltpu.SMEM(diffusivity.shape, f32),
            pltpu.SemaphoreType.DMA((3, 3)),
            pltpu.SemaphoreType.DMA((2, 4, vectors)),
            pltpu.SemaphoreType.DMA((2, 4, vectors)),
            pltpu.SemaphoreType.DMA((2, states)),
            pltpu.SemaphoreType.DMA((2, states)),
            pltpu.SemaphoreType.DMA((space,)),
            pltpu.SemaphoreType.DMA((space,)),
        ],
        compiler_params=pltpu.CompilerParams(
            collective_id=0, has_side_effects=True, vmem_limit_bytes=48 * 1024 * 1024
        ),
        name="tangent_step",
    )(*[pltpu.with_memory_space_constraint(a, pltpu.HBM) for a in (tangents, background, diffusivity)])
    block = (vectors, 1, depth, ny, nx)
    return pl.pallas_call(
        functools.partial(basis_kernel, tangents[0].size * space),
        grid=(comps,),
        out_shape=(
            jax.ShapeDtypeStruct(tangents.shape, f32),
            jax.ShapeDtypeStruct((vectors, vectors), f32),
        ),
        in_specs=[vmem, vmem],
        out_specs=(pl.BlockSpec(block, lambda c: (0, c, 0, 0, 0)), vmem),
        compiler_params=pltpu.CompilerParams(vmem_limit_bytes=16 * 1024 * 1024),
        name="basis",
    )(stepped, coef)


def solution(mesh):
    in_specs = (
        P("member", None, "space", None, None),
        P("member", None, "space", None, None),
        P("member"),
    )
    out_specs = (P("member", None, "space", None, None), P("member", None))
    return jax.shard_map(
        on_device, mesh=mesh, in_specs=in_specs, out_specs=out_specs, check_vma=False
    )
```

```python
import functools
import jax
import jax.numpy as jnp
from jax import lax
from jax.experimental import pallas as pl
from jax.experimental.pallas import tpu as pltpu
from jax.sharding import PartitionSpec as P

STEP_DT = 0.25
BUOYANCY = 1.0
MESH = pl.DeviceIdType.MESH
PAD = 8
GROUP = 4
ROWS = 32
GRAM_ROWS = 16
PAIRS = [(i, j) for j in range(4) for i in range(j + 1)]


def step_kernel(
    space,
    t_hbm,
    b_hbm,
    diff_hbm,
    stepped,
    coef_out,
    y0,
    y1,
    y2,
    y3,
    base,
    base_lo,
    base_hi,
    lo,
    hi,
    coef,
    grams,
    diff,
    relay,
    base_relay,
    local_sem,
    send_sem,
    recv_sem,
    base_send,
    base_recv,
    gram_send,
    gram_recv,
    relay_send,
    relay_recv,
    base_relay_send,
    base_relay_recv,
):
    vectors, comps, depth, ny, nx = t_hbm.shape
    states = b_hbm.shape[0]
    last = depth - 1
    me = lax.axis_index("space")
    upper = lax.rem(me + 1, space)
    lower = lax.rem(me + space - 1, space)
    has_lower = me > 0
    has_upper = me < space - 1
    ys = [y0, y1, y2, y3]

    relays = space % GROUP == 0 and space <= GROUP * GROUP
    groups = max(space // GROUP, 1)
    group, seat = lax.div(me, GROUP), lax.rem(me, GROUP)

    def via_up(items):
        return lax.div(items * (groups - 1 - group), groups)

    def via_down(items):
        return lax.div(items * group, groups)

    def local_copies():
        out = []
        for k, (src, dst) in enumerate(((b_hbm, base), (t_hbm, y0))):
            for m, (a, b, rows) in enumerate(
                ((0, PAD, ny), (ny - PAD, 0, PAD), (0, PAD + ny, PAD))
            ):
                out.append(
                    pltpu.make_async_copy(
                        src.at[:, :, :, pl.ds(a, rows), :],
                        dst.at[:, :, :, pl.ds(b, rows), :],
                        local_sem.at[k, m],
                    )
                )
        return out

    def remote(src, dst, sems, device):
        return pltpu.make_async_remote_copy(
            src, dst, sems[0], sems[1], device_id={"space": device}, device_id_type=MESH
        )

    around = [lax.rem(me + space + k, space) for k in (-2, 2, 3, -3)]

    def base_up(b, via=False):
        dst, sem = (base_relay, base_relay_recv.at[b]) if via else (base_lo, base_recv.at[0, b])
        device = around[0] if via else upper
        return remote(b_hbm.at[b, :, last], dst.at[b], (base_send.at[0, b], sem), device)

    def base_down(b, via=False):
        dst, sem = (base_relay, base_relay_recv.at[b]) if via else (base_hi, base_recv.at[1, b])
        device = around[1] if via else lower
        return remote(b_hbm.at[b, :, 0], dst.at[b], (base_send.at[1, b], sem), device)

    def state_plane(s, j, p):
        if s == 0:
            return t_hbm.at[j, :, p]
        return ys[s].at[j, :, p, pl.ds(PAD, ny), :]

    def send_up(s, j, via=False):
        dst, sem = (relay, relay_recv.at[s, j]) if via else (lo, recv_sem.at[0, s, j])
        device = around[0] if via else upper
        return remote(
            state_plane(s, j, last), dst.at[s, j], (send_sem.at[0, s, j], sem), device
        )

    def send_down(s, j, via=False):
        dst, sem = (relay, relay_recv.at[s, j]) if via else (hi, recv_sem.at[1, s, j])
        device = around[1] if via else lower
        return remote(state_plane(s, j, 0), dst.at[s, j], (send_sem.at[1, s, j], sem), device)

    def start(up, down, *key):
        items = states if len(key) == 1 else vectors
        if relays:
            around_up = jnp.logical_and(seat == GROUP - 1, key[-1] < via_up(items))
            around_down = jnp.logical_and(seat == 0, key[-1] < via_down(items))

            @pl.when(around_up)
            def _():
                up(*key, via=True).start()

            @pl.when(around_down)
            def _():
                down(*key, via=True).start()

            straight_up = jnp.logical_and(has_upper, jnp.logical_not(around_up))
            straight_down = jnp.logical_and(has_lower, jnp.logical_not(around_down))
        else:
            straight_up, straight_down = has_upper, has_lower

        @pl.when(straight_up)
        def _():
            up(*key).start()

        @pl.when(straight_down)
        def _():
            down(*key).start()

    def passes(*key, op):
        if not relays:
            return
        if len(key) == 1:
            items, held, sends, arrivals = states, base_relay, base_relay_send, base_relay_recv
            ends, ends_recv = (base_lo, base_hi), base_recv
        else:
            items, held, sends, arrivals = vectors, relay, relay_send, relay_recv
            ends, ends_recv = (lo, hi), recv_sem
        for side, (place, count) in enumerate(((1, via_up(items)), (2, via_down(items)))):

            @pl.when(jnp.logical_and(seat == place, key[-1] < count))
            def _():
                src = held.at[key]
                onward = remote(
                    src, ends[side].at[key], (sends.at[key], ends_recv.at[(side, *key)]),
                    around[2 + side],
                )
                if op == "start":
                    remote(src, src, (sends.at[key], arrivals.at[key]), upper).wait_recv()
                    onward.start()
                else:
                    onward.wait_send()

    def sent(up, down, *key):
        @pl.when(has_upper)
        def _():
            up(*key).wait_send()

        @pl.when(has_lower)
        def _():
            down(*key).wait_send()

        passes(*key, op="wait_send")

    def receive(up, down, *key):
        passes(*key, op="start")

        @pl.when(has_lower)
        def _():
            up(*key).wait_recv()

        @pl.when(has_upper)
        def _():
            down(*key).wait_recv()

    copies = local_copies() + [pltpu.make_async_copy(diff_hbm, diff, local_sem.at[2, 0])]
    for c in copies:
        c.start()

    barrier = pltpu.get_barrier_semaphore()

    @pl.loop(1, space)
    def _(d):
        pl.semaphore_signal(
            barrier, inc=1, device_id={"space": lax.rem(me + d, space)}, device_id_type=MESH
        )

    pl.semaphore_wait(barrier, space - 1)

    start(base_up, base_down, 0)

    @pl.loop(0, vectors)
    def _(j):
        start(send_up, send_down, 0, j)

    start(base_up, base_down, 1)

    @pl.when(jnp.logical_not(has_lower))
    def _():
        base_lo[...] = jnp.zeros_like(base_lo)

        @pl.loop(0, vectors)
        def _(j):
            for s in range(4):
                lo[s, j] = jnp.zeros(lo.shape[2:], jnp.float32)

    @pl.when(jnp.logical_not(has_upper))
    def _():
        base_hi[...] = jnp.zeros_like(base_hi)

        @pl.loop(0, vectors)
        def _(j):
            for s in range(4):
                hi[s, j] = jnp.zeros(hi.shape[2:], jnp.float32)

    for c in copies:
        c.wait()
    nu, kappa = diff[0], diff[1]

    def x_sides(q):
        return pltpu.roll(q, nx - 1, 1), pltpu.roll(q, 1, 1)

    def base_coeffs(b, p):
        @pl.loop(0, ny, step=ROWS)
        def _(r):
            r = pl.multiple_of(r, ROWS)
            here = pl.ds(r, ROWS)
            for c in range(comps):
                q = base[b, c, p, pl.ds(PAD + r, ROWS), :]
                right, left = x_sides(q)
                front = base[b, c, p, pl.ds(PAD + 1 + r, ROWS), :]
                back = base[b, c, p, pl.ds(PAD - 1 + r, ROWS), :]
                if p == 0:
                    below = base_lo[b, c, here, :]
                else:
                    below = base[b, c, p - 1, pl.ds(PAD + r, ROWS), :]
                if p == last:
                    above = base_hi[b, c, here, :]
                else:
                    above = base[b, c, p + 1, pl.ds(PAD + r, ROWS), :]
                if c < 3:
                    coef[b, p, c, here, :] = -0.5 * q
                coef[b, p, 3 + 3 * c, here, :] = 0.5 * (left - right)
                coef[b, p, 4 + 3 * c, here, :] = 0.5 * (back - front)
                coef[b, p, 5 + 3 * c, here, :] = 0.5 * (below - above)

    def advance(s, b, j, p):
        y = ys[s]

        @pl.loop(0, ny, step=ROWS)
        def _(r):
            r = pl.multiple_of(r, ROWS)
            here = pl.ds(r, ROWS)
            mid = pl.ds(PAD + r, ROWS)
            qs = [y[j, c, p, mid, :] for c in range(comps)]
            flow = [coef[b, p, d, here, :] for d in range(3)]
            for c in range(comps):
                q = qs[c]
                right, left = x_sides(q)
                front = y[j, c, p, pl.ds(PAD + 1 + r, ROWS), :]
                back = y[j, c, p, pl.ds(PAD - 1 + r, ROWS), :]
                below = lo[s, j, c, here, :] if p == 0 else y[j, c, p - 1, mid, :]
                above = hi[s, j, c, here, :] if p == last else y[j, c, p + 1, mid, :]
                rate = (
                    flow[0] * (right - left) + flow[1] * (front - back) + flow[2] * (above - below)
                )
                for d in range(3):
                    rate = rate + qs[d] * coef[b, p, 3 + 3 * c + d, here, :]
                sides = (right + left) + (front + back) + (above + below)
                rate = rate + (kappa if c == 3 else nu) * (sides - 6.0 * q)
                if c == 2:
                    rate = rate + BUOYANCY * qs[3]
                if c == 3:
                    rate = rate + qs[2]
                if s < 3:
                    origin = q if s == 0 else y0[j, c, p, mid, :]
                    step = STEP_DT if s == 2 else STEP_DT * 0.5
                    ys[s + 1][j, c, p, mid, :] = origin + step * rate
                else:
                    sums = (
                        y1[j, c, p, mid, :] + 2.0 * y2[j, c, p, mid, :] + (q - y0[j, c, p, mid, :])
                    )
                    stepped[j, c, p, here, :] = (1.0 / 3.0) * sums + (STEP_DT / 6.0) * rate

        if s < 3:
            nxt = ys[s + 1]
            for c in range(comps):
                nxt[j, c, p, pl.ds(0, PAD), :] = nxt[j, c, p, pl.ds(ny, PAD), :]
                nxt[j, c, p, pl.ds(PAD + ny, PAD), :] = nxt[j, c, p, pl.ds(PAD, PAD), :]

    inside = range(1, last)
    outside = [0, last] if last > 0 else [0]

    for p in inside:
        base_coeffs(0, p)

    which = [0, 1, 1, 2]
    for s in range(4):
        early = s in (0, 3)
        if early:

            @pl.loop(0, vectors)
            def _(j):
                for p in inside:
                    advance(s, which[s], j, p)

        if s == 0:
            for b in range(1, states):
                for p in inside:
                    base_coeffs(b, p)
        if s != 2:
            receive(base_up, base_down, which[s])
            for p in outside:
                base_coeffs(which[s], p)

        @pl.loop(0, vectors)
        def _(j):
            receive(send_up, send_down, s, j)
            for p in outside:
                advance(s, which[s], j, p)
            if s < 3:
                start(send_up, send_down, s + 1, j)
            if not early:
                for p in inside:
                    advance(s, which[s], j, p)

        if s == 1:
            start(base_up, base_down, 2)

    zero = jnp.zeros((GRAM_ROWS, nx), jnp.float32)
    sums = (zero,) * len(PAIRS)
    for p in range(depth):
        def body(k, sums, p=p):
            r = pl.multiple_of(k * GRAM_ROWS, GRAM_ROWS)
            for c in range(comps):
                q = [stepped[j, c, p, pl.ds(r, GRAM_ROWS), :] for j in range(vectors)]
                sums = tuple(a + q[i] * q[j] for a, (i, j) in zip(sums, PAIRS))
            return sums

        sums = lax.fori_loop(0, ny // GRAM_ROWS, body, sums)
    lane = lax.broadcasted_iota(jnp.int32, (1, nx), 1)
    packed = jnp.zeros((1, nx), jnp.float32)
    for k, a in enumerate(sums):
        whole = jnp.sum(jnp.sum(a, axis=0, keepdims=True), axis=1, keepdims=True)
        packed = jnp.where(lane == k, whole, packed)
    grams[me] = packed

    def gram_copy(d):
        return pltpu.make_async_remote_copy(
            grams.at[me], grams.at[me], gram_send.at[d], gram_recv.at[d],
            device_id={"space": lax.rem(me + d, space)}, device_id_type=MESH,
        )

    def gram_arrival(d):
        source = lax.rem(me + space - d, space)
        return pltpu.make_async_remote_copy(
            grams.at[source], grams.at[source], gram_send.at[d], gram_recv.at[d],
            device_id={"space": lax.rem(me + d, space)}, device_id_type=MESH,
        )

    @pl.loop(1, space)
    def _(d):
        gram_copy(d).start()

    @pl.loop(1, space)
    def _(d):
        gram_arrival(d).wait_recv()

    total = lax.fori_loop(0, space, lambda d, a: a + grams[d], jnp.zeros((1, nx), jnp.float32))
    gram = {
        pair: jnp.broadcast_to(
            jnp.sum(jnp.where(lane == k, total, 0.0), axis=1, keepdims=True), (1, nx)
        )
        for k, pair in enumerate(PAIRS)
    }

    low, inv = {}, {}
    recip = {}
    for k in range(vectors):
        rest = gram[k, k]
        for m in range(k):
            rest = rest - low[k, m] * low[k, m]
        low[k, k] = jnp.sqrt(rest)
        recip[k] = 1.0 / low[k, k]
        for i in range(k + 1, vectors):
            rest = gram[k, i]
            for m in range(k):
                rest = rest - low[i, m] * low[k, m]
            low[i, k] = rest * recip[k]
    for k in range(vectors):
        inv[k, k] = recip[k]
        for i in range(k + 1, vectors):
            rest = low[i, k] * inv[k, k]
            for m in range(k + 1, i):
                rest = rest + low[i, m] * inv[m, k]
            inv[i, k] = -rest * recip[i]
    blank = jnp.zeros((1, nx), jnp.float32)
    rows = [inv.get((i, k), blank) for i in range(vectors) for k in range(vectors)]
    rows += [low.get((k, i), blank) for i in range(vectors) for k in range(vectors)]
    coef_out[...] = jnp.concatenate(rows, axis=0)

    for b in range(states):
        sent(base_up, base_down, b)
    for s in range(4):
        @pl.loop(0, vectors)
        def _(j):
            sent(send_up, send_down, s, j)

    @pl.loop(1, space)
    def _(d):
        gram_copy(d).wait_send()


def basis_kernel(count, stepped, coef, basis, growth):
    vectors, _, depth, ny, nx = stepped.shape
    scale = jnp.sqrt(jnp.float32(count))
    comp = pl.program_id(0)

    def row(k):
        return jnp.broadcast_to(coef[k : k + 1, :], (8, nx))

    mix = {(i, k): scale * row(i * vectors + k) for i in range(vectors) for k in range(i + 1)}
    for p in range(depth):
        for r in range(0, ny, 8):
            q = [stepped[k, comp, p, r : r + 8, :] for k in range(vectors)]
            for i in range(vectors):
                total = mix[i, 0] * q[0]
                for k in range(1, i + 1):
                    total = total + mix[i, k] * q[k]
                basis[i, 0, p, r : r + 8, :] = total

    @pl.when(comp == 0)
    def _():
        lane = lax.broadcasted_iota(jnp.int32, (1, nx), 1)
        rows = []
        for i in range(vectors):
            out = jnp.zeros((1, nx), jnp.float32)
            for k in range(vectors):
                at = vectors * vectors + i * vectors + k
                out = jnp.where(lane == k, coef[at : at + 1, :], out)
            rows.append(out)
        growth[...] = (jnp.concatenate(rows, axis=0) / scale)[:, :vectors]


def on_device(tangents, background, diffusivity):
    space = lax.axis_size("space")
    vectors, comps, depth, ny, nx = tangents.shape
    states = background.shape[0]
    f32 = jnp.float32
    padded = ny + 2 * PAD
    vmem = pl.BlockSpec(memory_space=pltpu.VMEM)
    hbm = pl.BlockSpec(memory_space=pltpu.HBM)
    stepped, coef = pl.pallas_call(
        functools.partial(step_kernel, space),
        out_shape=(
            jax.ShapeDtypeStruct(tangents.shape, f32),
            jax.ShapeDtypeStruct((2 * vectors * vectors, nx), f32),
        ),
        in_specs=[hbm, hbm, hbm],
        out_specs=(vmem, vmem),
        scratch_shapes=[pltpu.VMEM((vectors, comps, depth, padded, nx), f32)] * 4
        + [
            pltpu.VMEM((states, comps, depth, padded, nx), f32),
            pltpu.VMEM((states, comps, ny, nx), f32),
            pltpu.VMEM((states, comps, ny, nx), f32),
            pltpu.VMEM((4, vectors, comps, ny, nx), f32),
            pltpu.VMEM((4, vectors, comps, ny, nx), f32),
            pltpu.VMEM((states, depth, 15, ny, nx), f32),
            pltpu.VMEM((space, 1, nx), f32),
            pltpu.SMEM(diffusivity.shape, f32),
            pltpu.VMEM((4, vectors, comps, ny, nx), f32),
            pltpu.VMEM((states, comps, ny, nx), f32),
            pltpu.SemaphoreType.DMA((3, 3)),
            pltpu.SemaphoreType.DMA((2, 4, vectors)),
            pltpu.SemaphoreType.DMA((2, 4, vectors)),
            pltpu.SemaphoreType.DMA((2, states)),
            pltpu.SemaphoreType.DMA((2, states)),
            pltpu.SemaphoreType.DMA((space,)),
            pltpu.SemaphoreType.DMA((space,)),
            pltpu.SemaphoreType.DMA((4, vectors)),
            pltpu.SemaphoreType.DMA((4, vectors)),
            pltpu.SemaphoreType.DMA((states,)),
            pltpu.SemaphoreType.DMA((states,)),
        ],
        compiler_params=pltpu.CompilerParams(
            collective_id=0, has_side_effects=True, vmem_limit_bytes=48 * 1024 * 1024
        ),
        name="tangent_step",
    )(*[pltpu.with_memory_space_constraint(a, pltpu.HBM) for a in (tangents, background, diffusivity)])
    block = (vectors, 1, depth, ny, nx)
    return pl.pallas_call(
        functools.partial(basis_kernel, tangents[0].size * space),
        grid=(comps,),
        out_shape=(
            jax.ShapeDtypeStruct(tangents.shape, f32),
            jax.ShapeDtypeStruct((vectors, vectors), f32),
        ),
        in_specs=[vmem, vmem],
        out_specs=(pl.BlockSpec(block, lambda c: (0, c, 0, 0, 0)), vmem),
        compiler_params=pltpu.CompilerParams(vmem_limit_bytes=16 * 1024 * 1024),
        name="basis",
    )(stepped, coef)


def solution(mesh):
    in_specs = (
        P("member", None, "space", None, None),
        P("member", None, "space", None, None),
        P("member"),
    )
    out_specs = (P("member", None, "space", None, None), P("member", None))
    return jax.shard_map(
        on_device, mesh=mesh, in_specs=in_specs, out_specs=out_specs, check_vma=False
    )
```

```python
import functools
import jax
import jax.numpy as jnp
from jax import lax
from jax.experimental import pallas as pl
from jax.experimental.pallas import tpu as pltpu
from jax.sharding import PartitionSpec as P

STEP_DT = 0.25
BUOYANCY = 1.0
MESH = pl.DeviceIdType.MESH
PAD = 8
GROUP = 4
ROWS = 32
GRAM_ROWS = 16
PAIRS = [(i, j) for j in range(4) for i in range(j + 1)]


def step_kernel(
    space,
    t_hbm,
    b_hbm,
    diff_hbm,
    stepped,
    coef_out,
    y0,
    y1,
    y2,
    y3,
    base,
    base_lo,
    base_hi,
    lo,
    hi,
    coef,
    grams,
    diff,
    relay,
    base_relay,
    local_sem,
    send_sem,
    recv_sem,
    base_send,
    base_recv,
    gram_send,
    gram_recv,
    relay_send,
    relay_recv,
    base_relay_send,
    base_relay_recv,
):
    vectors, comps, depth, ny, nx = t_hbm.shape
    states = b_hbm.shape[0]
    last = depth - 1
    me = lax.axis_index("space")
    upper = lax.rem(me + 1, space)
    lower = lax.rem(me + space - 1, space)
    has_lower = me > 0
    has_upper = me < space - 1
    ys = [y0, y1, y2, y3]

    relays = space % GROUP == 0 and space <= GROUP * GROUP
    groups = max(space // GROUP, 1)
    group, seat = lax.div(me, GROUP), lax.rem(me, GROUP)

    def via_up(items):
        return lax.div(items * (groups - 1 - group), groups)

    def via_down(items):
        return lax.div(items * group, groups)

    def local_copies():
        out = []
        for k, (src, dst) in enumerate(((b_hbm, base), (t_hbm, y0))):
            for m, (a, b, rows) in enumerate(
                ((0, PAD, ny), (ny - PAD, 0, PAD), (0, PAD + ny, PAD))
            ):
                out.append(
                    pltpu.make_async_copy(
                        src.at[:, :, :, pl.ds(a, rows), :],
                        dst.at[:, :, :, pl.ds(b, rows), :],
                        local_sem.at[k, m],
                    )
                )
        return out

    def remote(src, dst, sems, device):
        return pltpu.make_async_remote_copy(
            src, dst, sems[0], sems[1], device_id={"space": device}, device_id_type=MESH
        )

    around = [lax.rem(me + space + k, space) for k in (-2, 2, 3, -3)]

    def base_up(b, via=False):
        dst, sem = (base_relay, base_relay_recv.at[b]) if via else (base_lo, base_recv.at[0, b])
        device = around[0] if via else upper
        return remote(b_hbm.at[b, :, last], dst.at[b], (base_send.at[0, b], sem), device)

    def base_down(b, via=False):
        dst, sem = (base_relay, base_relay_recv.at[b]) if via else (base_hi, base_recv.at[1, b])
        device = around[1] if via else lower
        return remote(b_hbm.at[b, :, 0], dst.at[b], (base_send.at[1, b], sem), device)

    def state_plane(s, j, p):
        if s == 0:
            return t_hbm.at[j, :, p]
        return ys[s].at[j, :, p, pl.ds(PAD, ny), :]

    def send_up(s, j, via=False):
        dst, sem = (relay, relay_recv.at[s, j]) if via else (lo, recv_sem.at[0, s, j])
        device = around[0] if via else upper
        return remote(
            state_plane(s, j, last), dst.at[s, j], (send_sem.at[0, s, j], sem), device
        )

    def send_down(s, j, via=False):
        dst, sem = (relay, relay_recv.at[s, j]) if via else (hi, recv_sem.at[1, s, j])
        device = around[1] if via else lower
        return remote(state_plane(s, j, 0), dst.at[s, j], (send_sem.at[1, s, j], sem), device)

    def start(up, down, *key):
        items = states if len(key) == 1 else vectors
        if relays:
            around_up = jnp.logical_and(seat == GROUP - 1, key[-1] < via_up(items))
            around_down = jnp.logical_and(seat == 0, key[-1] < via_down(items))

            @pl.when(around_up)
            def _():
                up(*key, via=True).start()

            @pl.when(around_down)
            def _():
                down(*key, via=True).start()

            straight_up = jnp.logical_and(has_upper, jnp.logical_not(around_up))
            straight_down = jnp.logical_and(has_lower, jnp.logical_not(around_down))
        else:
            straight_up, straight_down = has_upper, has_lower

        @pl.when(straight_up)
        def _():
            up(*key).start()

        @pl.when(straight_down)
        def _():
            down(*key).start()

    def passes(*key, op):
        if not relays:
            return
        if len(key) == 1:
            items, held, sends, arrivals = states, base_relay, base_relay_send, base_relay_recv
            ends, ends_recv = (base_lo, base_hi), base_recv
        else:
            items, held, sends, arrivals = vectors, relay, relay_send, relay_recv
            ends, ends_recv = (lo, hi), recv_sem
        for side, (place, count) in enumerate(((1, via_up(items)), (2, via_down(items)))):

            @pl.when(jnp.logical_and(seat == place, key[-1] < count))
            def _():
                src = held.at[key]
                onward = remote(
                    src, ends[side].at[key], (sends.at[key], ends_recv.at[(side, *key)]),
                    around[2 + side],
                )
                if op == "start":
                    remote(src, src, (sends.at[key], arrivals.at[key]), upper).wait_recv()
                    onward.start()
                else:
                    onward.wait_send()

    def sent(up, down, *key):
        @pl.when(has_upper)
        def _():
            up(*key).wait_send()

        @pl.when(has_lower)
        def _():
            down(*key).wait_send()

        passes(*key, op="wait_send")

    def receive(up, down, *key):
        passes(*key, op="start")

        @pl.when(has_lower)
        def _():
            up(*key).wait_recv()

        @pl.when(has_upper)
        def _():
            down(*key).wait_recv()

    copies = local_copies() + [pltpu.make_async_copy(diff_hbm, diff, local_sem.at[2, 0])]
    for c in copies:
        c.start()

    barrier = pltpu.get_barrier_semaphore()

    @pl.loop(1, space)
    def _(d):
        pl.semaphore_signal(
            barrier, inc=1, device_id={"space": lax.rem(me + d, space)}, device_id_type=MESH
        )

    pl.semaphore_wait(barrier, space - 1)

    start(base_up, base_down, 0)

    @pl.loop(0, vectors)
    def _(j):
        start(send_up, send_down, 0, j)

    @pl.when(jnp.logical_not(has_lower))
    def _():
        base_lo[...] = jnp.zeros_like(base_lo)

        @pl.loop(0, vectors)
        def _(j):
            for s in range(4):
                lo[s, j] = jnp.zeros(lo.shape[2:], jnp.float32)

    @pl.when(jnp.logical_not(has_upper))
    def _():
        base_hi[...] = jnp.zeros_like(base_hi)

        @pl.loop(0, vectors)
        def _(j):
            for s in range(4):
                hi[s, j] = jnp.zeros(hi.shape[2:], jnp.float32)

    for c in copies:
        c.wait()
    nu, kappa = diff[0], diff[1]

    def x_sides(q):
        return pltpu.roll(q, nx - 1, 1), pltpu.roll(q, 1, 1)

    def base_coeffs(b, p):
        @pl.loop(0, ny, step=ROWS)
        def _(r):
            r = pl.multiple_of(r, ROWS)
            here = pl.ds(r, ROWS)
            for c in range(comps):
                q = base[b, c, p, pl.ds(PAD + r, ROWS), :]
                right, left = x_sides(q)
                front = base[b, c, p, pl.ds(PAD + 1 + r, ROWS), :]
                back = base[b, c, p, pl.ds(PAD - 1 + r, ROWS), :]
                if p == 0:
                    below = base_lo[b, c, here, :]
                else:
                    below = base[b, c, p - 1, pl.ds(PAD + r, ROWS), :]
                if p == last:
                    above = base_hi[b, c, here, :]
                else:
                    above = base[b, c, p + 1, pl.ds(PAD + r, ROWS), :]
                if c < 3:
                    coef[b, p, c, here, :] = -0.5 * q
                coef[b, p, 3 + 3 * c, here, :] = 0.5 * (left - right)
                coef[b, p, 4 + 3 * c, here, :] = 0.5 * (back - front)
                coef[b, p, 5 + 3 * c, here, :] = 0.5 * (below - above)

    def advance(s, b, j, p):
        y = ys[s]

        @pl.loop(0, ny, step=ROWS)
        def _(r):
            r = pl.multiple_of(r, ROWS)
            here = pl.ds(r, ROWS)
            mid = pl.ds(PAD + r, ROWS)
            qs = [y[j, c, p, mid, :] for c in range(comps)]
            flow = [coef[b, p, d, here, :] for d in range(3)]
            for c in range(comps):
                q = qs[c]
                right, left = x_sides(q)
                front = y[j, c, p, pl.ds(PAD + 1 + r, ROWS), :]
                back = y[j, c, p, pl.ds(PAD - 1 + r, ROWS), :]
                below = lo[s, j, c, here, :] if p == 0 else y[j, c, p - 1, mid, :]
                above = hi[s, j, c, here, :] if p == last else y[j, c, p + 1, mid, :]
                rate = (
                    flow[0] * (right - left) + flow[1] * (front - back) + flow[2] * (above - below)
                )
                for d in range(3):
                    rate = rate + qs[d] * coef[b, p, 3 + 3 * c + d, here, :]
                sides = (right + left) + (front + back) + (above + below)
                rate = rate + (kappa if c == 3 else nu) * (sides - 6.0 * q)
                if c == 2:
                    rate = rate + BUOYANCY * qs[3]
                if c == 3:
                    rate = rate + qs[2]
                if s < 3:
                    origin = q if s == 0 else y0[j, c, p, mid, :]
                    step = STEP_DT if s == 2 else STEP_DT * 0.5
                    ys[s + 1][j, c, p, mid, :] = origin + step * rate
                else:
                    sums = (
                        y1[j, c, p, mid, :] + 2.0 * y2[j, c, p, mid, :] + (q - y0[j, c, p, mid, :])
                    )
                    stepped[j, c, p, here, :] = (1.0 / 3.0) * sums + (STEP_DT / 6.0) * rate

        if s < 3:
            nxt = ys[s + 1]
            for c in range(comps):
                nxt[j, c, p, pl.ds(0, PAD), :] = nxt[j, c, p, pl.ds(ny, PAD), :]
                nxt[j, c, p, pl.ds(PAD + ny, PAD), :] = nxt[j, c, p, pl.ds(PAD, PAD), :]

    inside = range(1, last)
    outside = [0, last] if last > 0 else [0]

    for p in inside:
        base_coeffs(0, p)

    which = [0, 1, 1, 2]
    for s in range(4):
        early = s in (0, 3)
        if early:

            @pl.loop(0, vectors)
            def _(j):
                for p in inside:
                    advance(s, which[s], j, p)

        if s == 0:
            for b in range(1, states):
                for p in inside:
                    base_coeffs(b, p)
            start(base_up, base_down, 1)
        if s != 2:
            receive(base_up, base_down, which[s])
            for p in outside:
                base_coeffs(which[s], p)

        @pl.loop(0, vectors if s < 3 else vectors - 1)
        def _(j):
            receive(send_up, send_down, s, j)
            for p in outside:
                advance(s, which[s], j, p)
            if s < 3:
                start(send_up, send_down, s + 1, j)
            if not early:
                for p in inside:
                    advance(s, which[s], j, p)

        if s == 1:
            start(base_up, base_down, 2)

    def inner_products(planes, pairs, sums):
        for p in planes:

            def body(k, sums, p=p):
                r = pl.multiple_of(k * GRAM_ROWS, GRAM_ROWS)
                for c in range(comps):
                    used = sorted({j for pair in pairs for j in pair})
                    q = {j: stepped[j, c, p, pl.ds(r, GRAM_ROWS), :] for j in used}
                    sums = tuple(a + q[i] * q[j] for a, (i, j) in zip(sums, pairs))
                return sums

            sums = lax.fori_loop(0, ny // GRAM_ROWS, body, sums)
        return sums

    zero = jnp.zeros((GRAM_ROWS, nx), jnp.float32)
    first = [pair for pair in PAIRS if pair[1] < vectors - 1]
    final = [pair for pair in PAIRS if pair[1] == vectors - 1]
    sums = inner_products(range(depth), first, (zero,) * len(first))
    late = inner_products(inside, final, (zero,) * len(final))
    receive(send_up, send_down, 3, vectors - 1)
    for p in outside:
        advance(3, which[3], vectors - 1, p)
    sums = sums + inner_products(outside, final, late)

    lane = lax.broadcasted_iota(jnp.int32, (1, nx), 1)
    packed = jnp.zeros((1, nx), jnp.float32)
    for k, a in enumerate(sums):
        whole = jnp.sum(jnp.sum(a, axis=0, keepdims=True), axis=1, keepdims=True)
        packed = jnp.where(lane == k, whole, packed)
    grams[me] = packed

    def gram_copy(d):
        return pltpu.make_async_remote_copy(
            grams.at[me], grams.at[me], gram_send.at[d], gram_recv.at[d],
            device_id={"space": lax.rem(me + d, space)}, device_id_type=MESH,
        )

    def gram_arrival(d):
        source = lax.rem(me + space - d, space)
        return pltpu.make_async_remote_copy(
            grams.at[source], grams.at[source], gram_send.at[d], gram_recv.at[d],
            device_id={"space": lax.rem(me + d, space)}, device_id_type=MESH,
        )

    @pl.loop(1, space)
    def _(d):
        gram_copy(d).start()

    @pl.loop(1, space)
    def _(d):
        gram_arrival(d).wait_recv()

    total = lax.fori_loop(0, space, lambda d, a: a + grams[d], jnp.zeros((1, nx), jnp.float32))
    gram = {
        pair: jnp.broadcast_to(
            jnp.sum(jnp.where(lane == k, total, 0.0), axis=1, keepdims=True), (1, nx)
        )
        for k, pair in enumerate(PAIRS)
    }

    low, inv = {}, {}
    recip = {}
    for k in range(vectors):
        rest = gram[k, k]
        for m in range(k):
            rest = rest - low[k, m] * low[k, m]
        low[k, k] = jnp.sqrt(rest)
        recip[k] = 1.0 / low[k, k]
        for i in range(k + 1, vectors):
            rest = gram[k, i]
            for m in range(k):
                rest = rest - low[i, m] * low[k, m]
            low[i, k] = rest * recip[k]
    for k in range(vectors):
        inv[k, k] = recip[k]
        for i in range(k + 1, vectors):
            rest = low[i, k] * inv[k, k]
            for m in range(k + 1, i):
                rest = rest + low[i, m] * inv[m, k]
            inv[i, k] = -rest * recip[i]
    blank = jnp.zeros((1, nx), jnp.float32)
    rows = [inv.get((i, k), blank) for i in range(vectors) for k in range(vectors)]
    rows += [low.get((k, i), blank) for i in range(vectors) for k in range(vectors)]
    coef_out[...] = jnp.concatenate(rows, axis=0)

    for b in range(states):
        sent(base_up, base_down, b)
    for s in range(4):
        @pl.loop(0, vectors)
        def _(j):
            sent(send_up, send_down, s, j)

    @pl.loop(1, space)
    def _(d):
        gram_copy(d).wait_send()


def basis_kernel(count, stepped, coef, basis, growth):
    vectors, _, depth, ny, nx = stepped.shape
    scale = jnp.sqrt(jnp.float32(count))
    comp = pl.program_id(0)

    def row(k):
        return jnp.broadcast_to(coef[k : k + 1, :], (8, nx))

    mix = {(i, k): scale * row(i * vectors + k) for i in range(vectors) for k in range(i + 1)}
    for p in range(depth):
        for r in range(0, ny, 8):
            q = [stepped[k, comp, p, r : r + 8, :] for k in range(vectors)]
            for i in range(vectors):
                total = mix[i, 0] * q[0]
                for k in range(1, i + 1):
                    total = total + mix[i, k] * q[k]
                basis[i, 0, p, r : r + 8, :] = total

    @pl.when(comp == 0)
    def _():
        lane = lax.broadcasted_iota(jnp.int32, (1, nx), 1)
        rows = []
        for i in range(vectors):
            out = jnp.zeros((1, nx), jnp.float32)
            for k in range(vectors):
                at = vectors * vectors + i * vectors + k
                out = jnp.where(lane == k, coef[at : at + 1, :], out)
            rows.append(out)
        growth[...] = (jnp.concatenate(rows, axis=0) / scale)[:, :vectors]


def on_device(tangents, background, diffusivity):
    space = lax.axis_size("space")
    vectors, comps, depth, ny, nx = tangents.shape
    states = background.shape[0]
    f32 = jnp.float32
    padded = ny + 2 * PAD
    vmem = pl.BlockSpec(memory_space=pltpu.VMEM)
    hbm = pl.BlockSpec(memory_space=pltpu.HBM)
    stepped, coef = pl.pallas_call(
        functools.partial(step_kernel, space),
        out_shape=(
            jax.ShapeDtypeStruct(tangents.shape, f32),
            jax.ShapeDtypeStruct((2 * vectors * vectors, nx), f32),
        ),
        in_specs=[hbm, hbm, hbm],
        out_specs=(vmem, vmem),
        scratch_shapes=[pltpu.VMEM((vectors, comps, depth, padded, nx), f32)] * 4
        + [
            pltpu.VMEM((states, comps, depth, padded, nx), f32),
            pltpu.VMEM((states, comps, ny, nx), f32),
            pltpu.VMEM((states, comps, ny, nx), f32),
            pltpu.VMEM((4, vectors, comps, ny, nx), f32),
            pltpu.VMEM((4, vectors, comps, ny, nx), f32),
            pltpu.VMEM((states, depth, 15, ny, nx), f32),
            pltpu.VMEM((space, 1, nx), f32),
            pltpu.SMEM(diffusivity.shape, f32),
            pltpu.VMEM((4, vectors, comps, ny, nx), f32),
            pltpu.VMEM((states, comps, ny, nx), f32),
            pltpu.SemaphoreType.DMA((3, 3)),
            pltpu.SemaphoreType.DMA((2, 4, vectors)),
            pltpu.SemaphoreType.DMA((2, 4, vectors)),
            pltpu.SemaphoreType.DMA((2, states)),
            pltpu.SemaphoreType.DMA((2, states)),
            pltpu.SemaphoreType.DMA((space,)),
            pltpu.SemaphoreType.DMA((space,)),
            pltpu.SemaphoreType.DMA((4, vectors)),
            pltpu.SemaphoreType.DMA((4, vectors)),
            pltpu.SemaphoreType.DMA((states,)),
            pltpu.SemaphoreType.DMA((states,)),
        ],
        compiler_params=pltpu.CompilerParams(
            collective_id=0, has_side_effects=True, vmem_limit_bytes=48 * 1024 * 1024
        ),
        name="tangent_step",
    )(*[pltpu.with_memory_space_constraint(a, pltpu.HBM) for a in (tangents, background, diffusivity)])
    block = (vectors, 1, depth, ny, nx)
    return pl.pallas_call(
        functools.partial(basis_kernel, tangents[0].size * space),
        grid=(comps,),
        out_shape=(
            jax.ShapeDtypeStruct(tangents.shape, f32),
            jax.ShapeDtypeStruct((vectors, vectors), f32),
        ),
        in_specs=[vmem, vmem],
        out_specs=(pl.BlockSpec(block, lambda c: (0, c, 0, 0, 0)), vmem),
        compiler_params=pltpu.CompilerParams(vmem_limit_bytes=16 * 1024 * 1024),
        name="basis",
    )(stepped, coef)


def solution(mesh):
    in_specs = (
        P("member", None, "space", None, None),
        P("member", None, "space", None, None),
        P("member"),
    )
    out_specs = (P("member", None, "space", None, None), P("member", None))
    return jax.shard_map(
        on_device, mesh=mesh, in_specs=in_specs, out_specs=out_specs, check_vma=False
    )
```

```python
import functools
import jax
import jax.numpy as jnp
from jax import lax
from jax.experimental import pallas as pl
from jax.experimental.pallas import tpu as pltpu
from jax.sharding import PartitionSpec as P

STEP_DT = 0.25
BUOYANCY = 1.0
MESH = pl.DeviceIdType.MESH
PAD = 8
GROUP = 4
ROWS = 32
GRAM_ROWS = 16
PAIRS = [(i, j) for j in range(4) for i in range(j + 1)]


def step_kernel(
    space,
    t_hbm,
    b_hbm,
    diff_hbm,
    stepped,
    coef_out,
    y0,
    y1,
    y2,
    y3,
    base,
    base_lo,
    base_hi,
    lo,
    hi,
    coef,
    grams,
    diff,
    relay,
    base_relay,
    local_sem,
    send_sem,
    recv_sem,
    base_send,
    base_recv,
    gram_send,
    gram_recv,
    relay_send,
    relay_recv,
    base_relay_send,
    base_relay_recv,
):
    vectors, comps, depth, ny, nx = t_hbm.shape
    states = b_hbm.shape[0]
    last = depth - 1
    me = lax.axis_index("space")
    upper = lax.rem(me + 1, space)
    lower = lax.rem(me + space - 1, space)
    has_lower = me > 0
    has_upper = me < space - 1
    ys = [y0, y1, y2, y3]

    relays = space % GROUP == 0 and space <= GROUP * GROUP
    groups = max(space // GROUP, 1)
    group, seat = lax.div(me, GROUP), lax.rem(me, GROUP)

    def via_up(items):
        return lax.div(items * (groups - 1 - group), groups)

    def via_down(items):
        return lax.div(items * group, groups)

    def local_copies():
        out = []
        for k, (src, dst) in enumerate(((b_hbm, base), (t_hbm, y0))):
            for m, (a, b, rows) in enumerate(
                ((0, PAD, ny), (ny - PAD, 0, PAD), (0, PAD + ny, PAD))
            ):
                out.append(
                    pltpu.make_async_copy(
                        src.at[:, :, :, pl.ds(a, rows), :],
                        dst.at[:, :, :, pl.ds(b, rows), :],
                        local_sem.at[k, m],
                    )
                )
        return out

    def remote(src, dst, sems, device):
        return pltpu.make_async_remote_copy(
            src, dst, sems[0], sems[1], device_id={"space": device}, device_id_type=MESH
        )

    around = [lax.rem(me + space + k, space) for k in (-2, 2, 3, -3)]

    def base_up(b, via=False):
        dst, sem = (base_relay, base_relay_recv.at[b]) if via else (base_lo, base_recv.at[0, b])
        device = around[0] if via else upper
        return remote(b_hbm.at[b, :, last], dst.at[b], (base_send.at[0, b], sem), device)

    def base_down(b, via=False):
        dst, sem = (base_relay, base_relay_recv.at[b]) if via else (base_hi, base_recv.at[1, b])
        device = around[1] if via else lower
        return remote(b_hbm.at[b, :, 0], dst.at[b], (base_send.at[1, b], sem), device)

    def state_plane(s, j, p):
        if s == 0:
            return t_hbm.at[j, :, p]
        return ys[s].at[j, :, p, pl.ds(PAD, ny), :]

    def send_up(s, j, via=False):
        dst, sem = (relay, relay_recv.at[s, j]) if via else (lo, recv_sem.at[0, s, j])
        device = around[0] if via else upper
        return remote(
            state_plane(s, j, last), dst.at[s, j], (send_sem.at[0, s, j], sem), device
        )

    def send_down(s, j, via=False):
        dst, sem = (relay, relay_recv.at[s, j]) if via else (hi, recv_sem.at[1, s, j])
        device = around[1] if via else lower
        return remote(state_plane(s, j, 0), dst.at[s, j], (send_sem.at[1, s, j], sem), device)

    def start(up, down, *key, sides=("up", "down")):
        items = states if len(key) == 1 else vectors
        if relays:
            around_up = jnp.logical_and(seat == GROUP - 1, key[-1] < via_up(items))
            around_down = jnp.logical_and(seat == 0, key[-1] < via_down(items))

            if "up" in sides:

                @pl.when(around_up)
                def _():
                    up(*key, via=True).start()

            if "down" in sides:

                @pl.when(around_down)
                def _():
                    down(*key, via=True).start()

            straight_up = jnp.logical_and(has_upper, jnp.logical_not(around_up))
            straight_down = jnp.logical_and(has_lower, jnp.logical_not(around_down))
        else:
            straight_up, straight_down = has_upper, has_lower

        if "up" in sides:

            @pl.when(straight_up)
            def _():
                up(*key).start()

        if "down" in sides:

            @pl.when(straight_down)
            def _():
                down(*key).start()

    def passes(*key, op):
        if not relays:
            return
        if len(key) == 1:
            items, held, sends, arrivals = states, base_relay, base_relay_send, base_relay_recv
            ends, ends_recv = (base_lo, base_hi), base_recv
        else:
            items, held, sends, arrivals = vectors, relay, relay_send, relay_recv
            ends, ends_recv = (lo, hi), recv_sem
        for side, (place, count) in enumerate(((1, via_up(items)), (2, via_down(items)))):

            @pl.when(jnp.logical_and(seat == place, key[-1] < count))
            def _():
                src = held.at[key]
                onward = remote(
                    src, ends[side].at[key], (sends.at[key], ends_recv.at[(side, *key)]),
                    around[2 + side],
                )
                if op == "start":
                    remote(src, src, (sends.at[key], arrivals.at[key]), upper).wait_recv()
                    onward.start()
                else:
                    onward.wait_send()

    def sent(up, down, *key):
        @pl.when(has_upper)
        def _():
            up(*key).wait_send()

        @pl.when(has_lower)
        def _():
            down(*key).wait_send()

        passes(*key, op="wait_send")

    def receive_low(up, *key):
        @pl.when(has_lower)
        def _():
            up(*key).wait_recv()

    def receive_high(down, *key):
        @pl.when(has_upper)
        def _():
            down(*key).wait_recv()

    def receive(up, down, *key):
        passes(*key, op="start")
        receive_low(up, *key)
        receive_high(down, *key)

    copies = local_copies() + [pltpu.make_async_copy(diff_hbm, diff, local_sem.at[2, 0])]
    for c in copies:
        c.start()

    barrier = pltpu.get_barrier_semaphore()

    @pl.loop(1, space)
    def _(d):
        pl.semaphore_signal(
            barrier, inc=1, device_id={"space": lax.rem(me + d, space)}, device_id_type=MESH
        )

    pl.semaphore_wait(barrier, space - 1)

    start(base_up, base_down, 0)

    @pl.loop(0, vectors)
    def _(j):
        start(send_up, send_down, 0, j)

    @pl.when(jnp.logical_not(has_lower))
    def _():
        base_lo[...] = jnp.zeros_like(base_lo)

        @pl.loop(0, vectors)
        def _(j):
            for s in range(4):
                lo[s, j] = jnp.zeros(lo.shape[2:], jnp.float32)

    @pl.when(jnp.logical_not(has_upper))
    def _():
        base_hi[...] = jnp.zeros_like(base_hi)

        @pl.loop(0, vectors)
        def _(j):
            for s in range(4):
                hi[s, j] = jnp.zeros(hi.shape[2:], jnp.float32)

    for c in copies:
        c.wait()
    nu, kappa = diff[0], diff[1]

    def x_sides(q):
        return pltpu.roll(q, nx - 1, 1), pltpu.roll(q, 1, 1)

    def base_coeffs(b, p):
        @pl.loop(0, ny, step=ROWS)
        def _(r):
            r = pl.multiple_of(r, ROWS)
            here = pl.ds(r, ROWS)
            for c in range(comps):
                q = base[b, c, p, pl.ds(PAD + r, ROWS), :]
                right, left = x_sides(q)
                front = base[b, c, p, pl.ds(PAD + 1 + r, ROWS), :]
                back = base[b, c, p, pl.ds(PAD - 1 + r, ROWS), :]
                if p == 0:
                    below = base_lo[b, c, here, :]
                else:
                    below = base[b, c, p - 1, pl.ds(PAD + r, ROWS), :]
                if p == last:
                    above = base_hi[b, c, here, :]
                else:
                    above = base[b, c, p + 1, pl.ds(PAD + r, ROWS), :]
                if c < 3:
                    coef[b, p, c, here, :] = -0.5 * q
                coef[b, p, 3 + 3 * c, here, :] = 0.5 * (left - right)
                coef[b, p, 4 + 3 * c, here, :] = 0.5 * (back - front)
                coef[b, p, 5 + 3 * c, here, :] = 0.5 * (below - above)

    def advance(s, b, j, p):
        y = ys[s]

        @pl.loop(0, ny, step=ROWS)
        def _(r):
            r = pl.multiple_of(r, ROWS)
            here = pl.ds(r, ROWS)
            mid = pl.ds(PAD + r, ROWS)
            qs = [y[j, c, p, mid, :] for c in range(comps)]
            flow = [coef[b, p, d, here, :] for d in range(3)]
            for c in range(comps):
                q = qs[c]
                right, left = x_sides(q)
                front = y[j, c, p, pl.ds(PAD + 1 + r, ROWS), :]
                back = y[j, c, p, pl.ds(PAD - 1 + r, ROWS), :]
                below = lo[s, j, c, here, :] if p == 0 else y[j, c, p - 1, mid, :]
                above = hi[s, j, c, here, :] if p == last else y[j, c, p + 1, mid, :]
                rate = (
                    flow[0] * (right - left) + flow[1] * (front - back) + flow[2] * (above - below)
                )
                for d in range(3):
                    rate = rate + qs[d] * coef[b, p, 3 + 3 * c + d, here, :]
                sides = (right + left) + (front + back) + (above + below)
                rate = rate + (kappa if c == 3 else nu) * (sides - 6.0 * q)
                if c == 2:
                    rate = rate + BUOYANCY * qs[3]
                if c == 3:
                    rate = rate + qs[2]
                if s < 3:
                    origin = q if s == 0 else y0[j, c, p, mid, :]
                    step = STEP_DT if s == 2 else STEP_DT * 0.5
                    ys[s + 1][j, c, p, mid, :] = origin + step * rate
                else:
                    sums = (
                        y1[j, c, p, mid, :] + 2.0 * y2[j, c, p, mid, :] + (q - y0[j, c, p, mid, :])
                    )
                    stepped[j, c, p, here, :] = (1.0 / 3.0) * sums + (STEP_DT / 6.0) * rate

        if s < 3:
            nxt = ys[s + 1]
            for c in range(comps):
                nxt[j, c, p, pl.ds(0, PAD), :] = nxt[j, c, p, pl.ds(ny, PAD), :]
                nxt[j, c, p, pl.ds(PAD + ny, PAD), :] = nxt[j, c, p, pl.ds(PAD, PAD), :]

    inside = range(1, last)
    outside = [0, last] if last > 0 else [0]

    for p in inside:
        base_coeffs(0, p)

    which = [0, 1, 1, 2]

    def outer(s, j):
        if last == 0:
            receive(send_up, send_down, s, j)
            advance(s, which[s], j, 0)
            if s < 3:
                start(send_up, send_down, s + 1, j)
            return
        passes(s, j, op="start")
        receive_low(send_up, s, j)
        advance(s, which[s], j, 0)
        if s < 3:
            start(send_up, send_down, s + 1, j, sides=("down",))
        receive_high(send_down, s, j)
        advance(s, which[s], j, last)
        if s < 3:
            start(send_up, send_down, s + 1, j, sides=("up",))

    for s in range(4):
        early = s in (0, 3)
        if early:

            @pl.loop(0, vectors)
            def _(j):
                for p in inside:
                    advance(s, which[s], j, p)

        if s == 0:
            for b in range(1, states):
                for p in inside:
                    base_coeffs(b, p)
            start(base_up, base_down, 1)
        if s != 2:
            receive(base_up, base_down, which[s])
            for p in outside:
                base_coeffs(which[s], p)

        @pl.loop(0, vectors if s < 3 else vectors - 1)
        def _(j):
            outer(s, j)
            if not early:
                for p in inside:
                    advance(s, which[s], j, p)

        if s == 1:
            start(base_up, base_down, 2)

    def inner_products(planes, pairs, sums):
        for p in planes:

            def body(k, sums, p=p):
                r = pl.multiple_of(k * GRAM_ROWS, GRAM_ROWS)
                for c in range(comps):
                    used = sorted({j for pair in pairs for j in pair})
                    q = {j: stepped[j, c, p, pl.ds(r, GRAM_ROWS), :] for j in used}
                    sums = tuple(a + q[i] * q[j] for a, (i, j) in zip(sums, pairs))
                return sums

            sums = lax.fori_loop(0, ny // GRAM_ROWS, body, sums)
        return sums

    zero = jnp.zeros((GRAM_ROWS, nx), jnp.float32)
    first = [pair for pair in PAIRS if pair[1] < vectors - 1]
    final = [pair for pair in PAIRS if pair[1] == vectors - 1]
    sums = inner_products(range(depth), first, (zero,) * len(first))
    late = inner_products(inside, final, (zero,) * len(final))
    outer(3, vectors - 1)
    sums = sums + inner_products(outside, final, late)

    lane = lax.broadcasted_iota(jnp.int32, (1, nx), 1)
    packed = jnp.zeros((1, nx), jnp.float32)
    for k, a in enumerate(sums):
        whole = jnp.sum(jnp.sum(a, axis=0, keepdims=True), axis=1, keepdims=True)
        packed = jnp.where(lane == k, whole, packed)
    grams[me] = packed

    def gram_copy(d):
        return pltpu.make_async_remote_copy(
            grams.at[me], grams.at[me], gram_send.at[d], gram_recv.at[d],
            device_id={"space": lax.rem(me + d, space)}, device_id_type=MESH,
        )

    def gram_arrival(d):
        source = lax.rem(me + space - d, space)
        return pltpu.make_async_remote_copy(
            grams.at[source], grams.at[source], gram_send.at[d], gram_recv.at[d],
            device_id={"space": lax.rem(me + d, space)}, device_id_type=MESH,
        )

    @pl.loop(1, space)
    def _(d):
        gram_copy(d).start()

    @pl.loop(1, space)
    def _(d):
        gram_arrival(d).wait_recv()

    total = lax.fori_loop(0, space, lambda d, a: a + grams[d], jnp.zeros((1, nx), jnp.float32))
    gram = {
        pair: jnp.broadcast_to(
            jnp.sum(jnp.where(lane == k, total, 0.0), axis=1, keepdims=True), (1, nx)
        )
        for k, pair in enumerate(PAIRS)
    }

    low, inv = {}, {}
    recip = {}
    for k in range(vectors):
        rest = gram[k, k]
        for m in range(k):
            rest = rest - low[k, m] * low[k, m]
        low[k, k] = jnp.sqrt(rest)
        recip[k] = 1.0 / low[k, k]
        for i in range(k + 1, vectors):
            rest = gram[k, i]
            for m in range(k):
                rest = rest - low[i, m] * low[k, m]
            low[i, k] = rest * recip[k]
    for k in range(vectors):
        inv[k, k] = recip[k]
        for i in range(k + 1, vectors):
            rest = low[i, k] * inv[k, k]
            for m in range(k + 1, i):
                rest = rest + low[i, m] * inv[m, k]
            inv[i, k] = -rest * recip[i]
    blank = jnp.zeros((1, nx), jnp.float32)
    rows = [inv.get((i, k), blank) for i in range(vectors) for k in range(vectors)]
    rows += [low.get((k, i), blank) for i in range(vectors) for k in range(vectors)]
    coef_out[...] = jnp.concatenate(rows, axis=0)

    for b in range(states):
        sent(base_up, base_down, b)
    for s in range(4):
        @pl.loop(0, vectors)
        def _(j):
            sent(send_up, send_down, s, j)

    @pl.loop(1, space)
    def _(d):
        gram_copy(d).wait_send()


def basis_kernel(count, stepped, coef, basis, growth):
    vectors, _, depth, ny, nx = stepped.shape
    scale = jnp.sqrt(jnp.float32(count))
    comp = pl.program_id(0)

    def row(k):
        return jnp.broadcast_to(coef[k : k + 1, :], (8, nx))

    mix = {(i, k): scale * row(i * vectors + k) for i in range(vectors) for k in range(i + 1)}
    for p in range(depth):
        for r in range(0, ny, 8):
            q = [stepped[k, comp, p, r : r + 8, :] for k in range(vectors)]
            for i in range(vectors):
                total = mix[i, 0] * q[0]
                for k in range(1, i + 1):
                    total = total + mix[i, k] * q[k]
                basis[i, 0, p, r : r + 8, :] = total

    @pl.when(comp == 0)
    def _():
        lane = lax.broadcasted_iota(jnp.int32, (1, nx), 1)
        rows = []
        for i in range(vectors):
            out = jnp.zeros((1, nx), jnp.float32)
            for k in range(vectors):
                at = vectors * vectors + i * vectors + k
                out = jnp.where(lane == k, coef[at : at + 1, :], out)
            rows.append(out)
        growth[...] = (jnp.concatenate(rows, axis=0) / scale)[:, :vectors]


def on_device(tangents, background, diffusivity):
    space = lax.axis_size("space")
    vectors, comps, depth, ny, nx = tangents.shape
    states = background.shape[0]
    f32 = jnp.float32
    padded = ny + 2 * PAD
    vmem = pl.BlockSpec(memory_space=pltpu.VMEM)
    hbm = pl.BlockSpec(memory_space=pltpu.HBM)
    stepped, coef = pl.pallas_call(
        functools.partial(step_kernel, space),
        out_shape=(
            jax.ShapeDtypeStruct(tangents.shape, f32),
            jax.ShapeDtypeStruct((2 * vectors * vectors, nx), f32),
        ),
        in_specs=[hbm, hbm, hbm],
        out_specs=(vmem, vmem),
        scratch_shapes=[pltpu.VMEM((vectors, comps, depth, padded, nx), f32)] * 4
        + [
            pltpu.VMEM((states, comps, depth, padded, nx), f32),
            pltpu.VMEM((states, comps, ny, nx), f32),
            pltpu.VMEM((states, comps, ny, nx), f32),
            pltpu.VMEM((4, vectors, comps, ny, nx), f32),
            pltpu.VMEM((4, vectors, comps, ny, nx), f32),
            pltpu.VMEM((states, depth, 15, ny, nx), f32),
            pltpu.VMEM((space, 1, nx), f32),
            pltpu.SMEM(diffusivity.shape, f32),
            pltpu.VMEM((4, vectors, comps, ny, nx), f32),
            pltpu.VMEM((states, comps, ny, nx), f32),
            pltpu.SemaphoreType.DMA((3, 3)),
            pltpu.SemaphoreType.DMA((2, 4, vectors)),
            pltpu.SemaphoreType.DMA((2, 4, vectors)),
            pltpu.SemaphoreType.DMA((2, states)),
            pltpu.SemaphoreType.DMA((2, states)),
            pltpu.SemaphoreType.DMA((space,)),
            pltpu.SemaphoreType.DMA((space,)),
            pltpu.SemaphoreType.DMA((4, vectors)),
            pltpu.SemaphoreType.DMA((4, vectors)),
            pltpu.SemaphoreType.DMA((states,)),
            pltpu.SemaphoreType.DMA((states,)),
        ],
        compiler_params=pltpu.CompilerParams(
            collective_id=0, has_side_effects=True, vmem_limit_bytes=48 * 1024 * 1024
        ),
        name="tangent_step",
    )(*[pltpu.with_memory_space_constraint(a, pltpu.HBM) for a in (tangents, background, diffusivity)])
    block = (vectors, 1, depth, ny, nx)
    return pl.pallas_call(
        functools.partial(basis_kernel, tangents[0].size * space),
        grid=(comps,),
        out_shape=(
            jax.ShapeDtypeStruct(tangents.shape, f32),
            jax.ShapeDtypeStruct((vectors, vectors), f32),
        ),
        in_specs=[vmem, vmem],
        out_specs=(pl.BlockSpec(block, lambda c: (0, c, 0, 0, 0)), vmem),
        compiler_params=pltpu.CompilerParams(vmem_limit_bytes=16 * 1024 * 1024),
        name="basis",
    )(stepped, coef)


def solution(mesh):
    in_specs = (
        P("member", None, "space", None, None),
        P("member", None, "space", None, None),
        P("member"),
    )
    out_specs = (P("member", None, "space", None, None), P("member", None))
    return jax.shard_map(
        on_device, mesh=mesh, in_specs=in_specs, out_specs=out_specs, check_vma=False
    )
```
